32 devices in a mesh: groups: 2 (over y), tp: 8 (over z, x), dp: 2 (over core).
Axes of the slice: x: 2, y: 2, z: 4, core: 2. Of those that a mesh axis runs over, the one named last changes fastest.
Arguments:
- activations: bfloat16 [2048, 8192], P(('groups', 'dp'), 'tp'), parts along dimension 0, may hold values from -6 to 6
- gate_weight: bfloat16 [8192, 28672], P('dp', 'tp'), may hold values from -0.0625 to 0.0625
- up_weight: bfloat16 [8192, 28672], P('dp', 'tp'), may hold values from -0.0625 to 0.0625
- out_grad: bfloat16 [2048, 8192], P(('groups', 'dp'), 'tp'), parts along dimension 0, may hold values from -6 to 6
- proj_in: bfloat16 [28672, 64], P('tp'), may hold values from -0.03125 to 0.03125
- proj_out: bfloat16 [8192, 64], P('tp'), may hold values from -0.0625 to 0.0625
- prompt_len: int32 [64], P(('groups', 'dp')), parts along dimension 0, may hold values from 1 to 16
- query_sketch: bfloat16 [8192, 4096], P(('groups', 'tp')), parts along dimension 0, may hold values from -6 to 6
- refusal_label: int32 [8192], P(('groups', 'tp')), parts along dimension 0, may hold values from 0 to 1
Outputs:
- scores: float32 [64, 4096], P(('groups', 'dp'), 'tp'), parts along dimension 0
- refusal_score: float32 [64], P(('groups', 'dp')), parts along dimension 0
The draws below stay inside these ranges and needn't reach their ends.
There are 2 independent parts, one for each index of `groups`. The reference program is written for one: setup_inputs(seed, part) draws one part's arguments, and reference() takes and returns one part's arrays. A program takes and returns all parts, laid end to end along the dimension named above; an argument that names none is the same for every part. Nothing has to cross between parts.
All inputs are finite; a program needn't handle non-finite values.
Results may differ from the reference program's by a relative error of at most 0.0044.
Values may be sent and summed in bfloat16 or wider, within the bound.
A program may use at most 384 MiB of HBM per device.

```python
import jax
import jax.numpy as jnp
from jax import lax

D = 8192
FF = 28672
R = 64
SEQ = 32
NQ = 4096
TOKENS = 1024
EXAMPLES = 32


def place_ends(result, stream_key, least, high):
    extent = result.shape
    spot = [jax.random.randint(jax.random.fold_in(stream_key, axis), (), 0, extent[axis]) for axis in range(len(extent))]
    result = result.at[tuple(spot)].set(least)
    longest = extent.index(max(extent))
    spot[longest] = (spot[longest] + 1) % extent[longest]
    return result.at[tuple(spot)].set(high)


def block_scale(stream_key, shape, split, low, high):
    def one(axis_at, shards_of):
        steps = jax.random.uniform(jax.random.fold_in(jax.random.fold_in(stream_key, 6), axis_at), (shards_of,), jnp.float32, low / len(split), high / len(split))
        return jnp.repeat(jnp.exp(steps), shape[axis_at] // shards_of).reshape((-1,) + (1,) * (len(shape) - axis_at - 1))

    factor_of = one(*split[0])
    for cut in split[1:]:
        factor_of = factor_of * one(*cut)
    return factor_of


def gaussian(key, dims, deviation, bound, cuts=(), held_as=jnp.bfloat16):
    drawn = deviation * jax.random.normal(key, dims, jnp.float32)
    if cuts:
        drawn = drawn * block_scale(key, dims, cuts, -0.22, 0.18)
    return jnp.clip(drawn, -bound, bound).astype(held_as)


def setup_inputs(seed: int = 0, part: int = 0) -> dict:
    keys = jax.random.split(jax.random.key(seed), 10)
    part_splits = jax.random.split(jax.random.fold_in(keys[9], part), 10)
    activations = gaussian(part_splits[0], (TOKENS, D), 1.0, 6.0, ((0, 2), (1, 8)))
    gate_weight = gaussian(keys[1], (D, FF), D ** -0.5, 0.0625, ((0, 2), (1, 8)))
    up_weight = gaussian(keys[2], (D, FF), D ** -0.5, 0.0625, ((0, 2), (1, 8)))
    out_grad = gaussian(part_splits[3], (TOKENS, D), 1.0, 6.0, ((0, 2), (1, 8)))
    proj_in = gaussian(keys[4], (FF, R), FF ** -0.5, 0.03125, ((0, 8),))
    proj_out = gaussian(keys[5], (D, R), D ** -0.5, 0.0625, ((0, 8),))
    prompt_len = place_ends(jax.random.randint(part_splits[6], (EXAMPLES,), 1, SEQ // 2 + 1), jax.random.fold_in(part_splits[6], 1), 1, (SEQ // 2 + 1) - 1).astype(jnp.int32)
    query_sketch = gaussian(part_splits[7], (NQ, R * R), 1.0, 6.0, ((0, 8),))
    refusal_label = place_ends(jax.random.randint(part_splits[8], (NQ,), 0, 2), jax.random.fold_in(part_splits[8], 1), 0, 1).astype(jnp.int32)
    return dict(activations=activations, gate_weight=gate_weight, up_weight=up_weight, out_grad=out_grad, proj_in=proj_in, proj_out=proj_out, prompt_len=prompt_len, query_sketch=query_sketch, refusal_label=refusal_label)


def reference(activations, gate_weight, up_weight, out_grad, proj_in, proj_out, prompt_len, query_sketch, refusal_label):
    gate_sum = jnp.dot(activations, gate_weight, preferred_element_type=jnp.float32)
    up_sum = jnp.dot(activations, up_weight, preferred_element_type=jnp.float32)
    hidden = (jax.nn.silu(gate_sum) * up_sum).astype(jnp.bfloat16)
    in_side = jnp.dot(hidden, proj_in, preferred_element_type=jnp.float32)
    out_side = jnp.dot(out_grad, proj_out, preferred_element_type=jnp.float32)
    count = in_side.shape[0] // SEQ
    response = (jnp.arange(SEQ, dtype=jnp.int32)[None, :] >= prompt_len[:, None]).astype(jnp.float32)
    masked = out_side.reshape(count, SEQ, R) * response[:, :, None]
    sketch = jnp.einsum('eti,etj->eij', masked, in_side.reshape(count, SEQ, R), precision=lax.Precision.HIGHEST)
    sketch = sketch.reshape(count, R * R).astype(jnp.bfloat16)
    scores = lax.dot_general(sketch, query_sketch, (((1,), (1,)), ((), ())), preferred_element_type=jnp.float32) * (1.0 / (4.0 * R))
    label_sign = (2 * refusal_label - 1).astype(jnp.float32)
    refusal_score = jnp.dot(scores, label_sign, precision=lax.Precision.HIGHEST) / jnp.sqrt(jnp.float32(NQ))
    return (scores, refusal_score)
```

```python
import functools

import jax
import jax.numpy as jnp
from jax import lax
from jax.experimental import pallas as pl
from jax.experimental.pallas import tpu as pltpu
from jax.sharding import PartitionSpec as P

R = 64
SEQ = 32
NQ = 4096
MESH = pl.DeviceIdType.MESH
NB = 3


def layer_kernel(
    nt, tn, act, gate, up, pin, outw, vin,
    sk_out, v_out,
    A, acc, wbuf, sendb, part, rpart, skg, vbuf,
    rsem, xsem, zsem, isem, psem, wsem, dsem, esem, tsem, trsem, gsem, grsem, vsem, vrsem, free,
):
    rows, feat = act.shape
    pr = rows // 2
    g = lax.axis_index("groups")
    t = lax.axis_index("tp")
    h = lax.axis_index("dp")
    z = t // 2
    x = t % 2
    u = z + h * (3 - 2 * z)
    v1 = jnp.minimum(u, 1)
    peer = (g, t, 1 - h)
    own = pl.multiple_of(h * rows, rows)
    oth = pl.multiple_of((1 - h) * rows, rows)

    def at_u(uu, xx):
        return (g, 2 * (uu + h * (3 - 2 * uu)) + xx, h)

    def ring(d):
        return (g, lax.rem(t + d, 8), h)

    def wcopies(w):
        s, j = w // (2 * nt), lax.rem(w, nt)
        v = v1 + (s % 2) * (1 - 2 * v1)
        kz = v + h * (1 - 2 * v)
        kx = x + (s // 2) * (1 - 2 * x)
        r0 = pl.multiple_of((kz * 2 + kx) * feat, feat)
        c0 = pl.multiple_of(j * tn, tn)
        b = lax.rem(w, NB)
        return [
            pltpu.make_async_copy(
                m.at[pl.ds(r0, feat), pl.ds(c0, tn)],
                wbuf.at[b, :, pl.ds(i * tn, tn)],
                wsem.at[b, i],
            )
            for i, m in enumerate((gate, up))
        ]

    def wstart(w):
        for c in wcopies(w):
            c.start()

    for w in range(NB - 1):
        wstart(jnp.int32(w))

    barrier = pltpu.get_barrier_semaphore()
    for d in range(1, 8):
        pl.semaphore_signal(barrier, inc=1, device_id=ring(d), device_id_type=MESH)
    pl.semaphore_signal(barrier, inc=1, device_id=peer, device_id_type=MESH)
    pl.semaphore_wait(barrier, 8)

    def rcopy(src, dst, ss, rs, dev):
        return pltpu.make_async_remote_copy(
            src_ref=src, dst_ref=dst, send_sem=ss, recv_sem=rs, device_id=dev, device_id_type=MESH
        )

    def prow(p):
        half = (1 - h) + (p // 2) * (2 * h - 1)
        return pl.ds(pl.multiple_of(half * rows + (p % 2) * pr, pr), pr)

    def piece(s, p):
        return A.at[s, prow(p), :]

    inner = u <= 1

    def mine(i):
        return pltpu.make_async_copy(act.at[pl.ds(i * pr, pr), :], piece(0, 2 + i), rsem.at[0, 2 + i])

    def lend(i):
        dst = A.at[0, pl.ds(pl.multiple_of(h * rows + i * pr, pr), pr), :]
        return rcopy(act.at[pl.ds(i * pr, pr), :], dst, isem.at[i], rsem.at[0, i], peer)

    @pl.when(inner)
    def _():
        for i in range(2):
            mine(i).start()

    @pl.when(jnp.logical_not(inner))
    def _():
        for i in range(2):
            lend(i).start()

    def xfwd(s, p):
        return rcopy(
            piece(s, p), piece(s + 2, p), xsem.at[s, p], rsem.at[s + 2, p], at_u(u, 1 - x)
        )

    def zout(s, p):
        ds = jnp.where(u == 0, 1, 0) if s == 0 else 1
        return rcopy(piece(s, p), piece(ds, p), zsem.at[s, p], rsem.at[ds, p], at_u(u + 1, x))

    def zin(p):
        return rcopy(piece(0, p), piece(1, p), psem.at[p], rsem.at[1, p], at_u(u - 1, x))

    def out_ok(s):
        return (u <= 2) if s == 0 else jnp.logical_and(u >= 1, u <= 2)

    def arrived(s, p):
        rcopy(piece(s, p), piece(s, p), xsem.at[0, 0], rsem.at[s, p], peer).wait_recv()

    def forward(s, p):
        arrived(s, p)

        @pl.when(out_ok(s))
        def _():
            zout(s, p).start()

        if s == 0:

            @pl.when(u == 1)
            def _():
                zin(p).start()

        xfwd(s, p).start()

    for d in range(1, 8):
        rcopy(vin, vbuf.at[d], vsem.at[d], vrsem.at[d], ring(d)).start()

    part[...] = outw[...]

    def wready(w):
        for c in wcopies(w):
            c.wait()

        @pl.when(w + NB - 1 < 8 * nt)
        def _():
            wstart(w + NB - 1)

        return lax.rem(w, NB)

    def step(s, m):
        rs = pl.ds(own if m else oth, rows)

        def body(j, _):
            b = wready((2 * s + m) * nt + j)
            for i in range(2):
                cs = pl.ds(i * tn, tn)
                r = jnp.dot(A[s, rs, :], wbuf[b, :, cs], preferred_element_type=jnp.float32)
                if s == 0:
                    acc[j, rs, cs] = r
                else:
                    acc[j, rs, cs] += r
            return 0

        lax.fori_loop(0, nt, body, 0)

    def dsend(j):
        b = lax.rem(j, 2)
        return rcopy(
            sendb.at[b], acc.at[j, pl.ds(own, rows), :], dsem.at[b], esem.at[j], peer
        )

    for s in range(3):
        for m in range(2):
            for p in (2 * m, 2 * m + 1):
                (forward if s < 2 else arrived)(s, p)
            step(s, m)

    for p in range(2):
        arrived(3, p)

    def give(j, _):
        b = wready(6 * nt + j)
        sb = lax.rem(j, 2)

        @pl.when(j >= 2)
        def _():
            dsend(j - 2).wait_send()

        for i in range(2):
            cs = pl.ds(i * tn, tn)
            sendb[sb, :, cs] = acc[j, pl.ds(oth, rows), cs] + jnp.dot(
                A[3, pl.ds(oth, rows), :], wbuf[b, :, cs], preferred_element_type=jnp.float32
            )
        pl.semaphore_signal(free, inc=1, device_id=peer, device_id_type=MESH)
        pl.semaphore_wait(free, 1)
        dsend(j).start()
        return 0

    lax.fori_loop(0, nt, give, 0)
    for p in range(2, 4):
        arrived(3, p)

    def take(j, _):
        b = wready(7 * nt + j)
        half = []
        rcopy(
            sendb.at[0], acc.at[j, pl.ds(oth, rows), :], dsem.at[0], esem.at[j], peer
        ).wait_recv()
        for i in range(2):
            cs = pl.ds(i * tn, tn)
            r = jnp.dot(
                A[3, pl.ds(own, rows), :], wbuf[b, :, cs], preferred_element_type=jnp.float32
            )
            half.append(r + acc[j, pl.ds(own, rows), cs] + acc[j, pl.ds(oth, rows), cs])
        gs, us = half
        hid = (gs / (1.0 + jnp.exp(-gs)) * us).astype(jnp.bfloat16)
        pj = pin[pl.ds(pl.multiple_of(j * tn, tn), tn), :]
        part[...] += jnp.dot(hid, pj, preferred_element_type=jnp.float32)
        return 0

    lax.fori_loop(0, nt, take, 0)
    for j in range(nt - 2, nt):
        dsend(jnp.int32(j)).wait_send()

    share = rows // 8
    per = share // SEQ

    def scatter(d):
        dest = lax.rem(t + d, 8)
        src = part.at[pl.ds(pl.multiple_of(dest * share, share), share), :]
        return rcopy(src, rpart.at[d], tsem.at[d], trsem.at[d], ring(d))

    for d in range(1, 8):
        scatter(d).start()
    side = part[pl.ds(pl.multiple_of(t * share, share), share), :]
    for d in range(1, 8):
        scatter(d).wait_recv()
        side = side + rpart[d]
    for e in range(per):
        one = side[e * SEQ : (e + 1) * SEQ, :]
        gram = lax.dot_general(
            one, one, (((0,), (0,)), ((), ())),
            precision=lax.Precision.HIGHEST, preferred_element_type=jnp.float32,
        )
        skg[t * per + e] = gram[R:, :].astype(jnp.bfloat16)

    def spread(d):
        ref = skg.at[pl.ds(t * per, per)]
        return rcopy(ref, ref, gsem.at[d], grsem.at[d], ring(d))

    def landed(d):
        ref = skg.at[pl.ds(lax.rem(t + 8 - d, 8) * per, per)]
        rcopy(ref, ref, gsem.at[d], grsem.at[d], ring(d)).wait_recv()

    for d in range(1, 8):
        spread(d).start()
    total = vin[...]
    for d in range(1, 8):
        rcopy(vin, vbuf.at[d], vsem.at[d], vrsem.at[d], ring(d)).wait()
        total = total + vbuf[d]
    v_out[...] = total
    for s in range(2):
        for p in range(4):
            xfwd(s, p).wait_send()

            @pl.when(out_ok(s))
            def _():
                zout(s, p).wait_send()

            if s == 0:

                @pl.when(u == 1)
                def _():
                    zin(p).wait_send()

    @pl.when(jnp.logical_not(inner))
    def _():
        for i in range(2):
            lend(i).wait_send()

    for d in range(1, 8):
        scatter(d).wait_send()
    for d in range(1, 8):
        landed(d)
        spread(d).wait_send()
    sk_out[...] = skg[...]


def layer(act, gate, up, pin, outw, vin):
    rows, feat = act.shape
    ff = gate.shape[1]
    tn = 512
    nt = ff // tn
    count = rows // SEQ
    dma = pltpu.SemaphoreType.DMA
    vm = pl.BlockSpec(memory_space=pltpu.VMEM)
    hbm = pl.BlockSpec(memory_space=pl.ANY)
    return pl.pallas_call(
        functools.partial(layer_kernel, nt, tn),
        out_shape=(
            jax.ShapeDtypeStruct((count, R, 2 * R), jnp.bfloat16),
            jax.ShapeDtypeStruct(vin.shape, jnp.float32),
        ),
        in_specs=[hbm, hbm, hbm, vm, vm, vm],
        out_specs=(vm, vm),
        scratch_shapes=[
            pltpu.VMEM((4, 2 * rows, feat), jnp.bfloat16),
            pltpu.VMEM((nt, 2 * rows, 2 * tn), jnp.float32),
            pltpu.VMEM((NB, feat, 2 * tn), jnp.bfloat16),
            pltpu.VMEM((2, rows, 2 * tn), jnp.float32),
            pltpu.VMEM((rows, 2 * R), jnp.float32),
            pltpu.VMEM((8, rows // 8, 2 * R), jnp.float32),
            pltpu.VMEM((count, R, 2 * R), jnp.bfloat16),
            pltpu.VMEM((8,) + vin.shape, jnp.float32),
            dma((4, 4)), dma((2, 4)), dma((2, 4)), dma((2,)), dma((4,)), dma((NB, 2)),
            dma((2,)), dma((nt,)), dma((8,)), dma((8,)), dma((8,)), dma((8,)), dma((8,)), dma((8,)),
            pltpu.SemaphoreType.REGULAR,
        ],
        compiler_params=pltpu.CompilerParams(
            collective_id=0, has_side_effects=True, vmem_limit_bytes=58 * 1024 * 1024
        ),
        cost_estimate=pl.CostEstimate(
            flops=8 * rows * gate.shape[0] * ff, bytes_accessed=8 * gate.shape[0] * ff,
            transcendentals=rows * ff,
        ),
    )(act, gate, up, pin, outw, vin)


def shards(
    activations,
    gate_weight,
    up_weight,
    out_grad,
    proj_in,
    proj_out,
    prompt_len,
    query_sketch,
    refusal_label,
):
    count = activations.shape[0] // SEQ
    scaling = 1.0 / (4.0 * R)
    label_sign = (2 * refusal_label - 1).astype(jnp.bfloat16)
    response = (jnp.arange(SEQ, dtype=jnp.int32)[None, :] >= prompt_len[:, None]).astype(
        jnp.float32
    )
    wide_out = jnp.pad(proj_out, ((0, 0), (R, 0)))
    wide_in = jnp.pad(proj_in, ((0, 0), (0, R)))
    outw = jnp.dot(out_grad, wide_out, preferred_element_type=jnp.float32)
    outw = outw * response.reshape(-1, 1)
    vin = jnp.dot(label_sign[None, :], query_sketch, preferred_element_type=jnp.float32)
    sk, vsum = layer(
        activations, gate_weight, up_weight, wide_in, outw, vin.reshape(-1, 128)
    )
    sketch = sk[:, :, :R].reshape(count, R * R)
    scores = (
        lax.dot_general(
            sketch, query_sketch, (((1,), (1,)), ((), ())), preferred_element_type=jnp.float32
        )
        * scaling
    )
    refusal_score = jnp.sum(sketch.astype(jnp.float32) * vsum.reshape(1, R * R), axis=1)
    refusal_score = refusal_score * (scaling / NQ**0.5)
    return (scores, refusal_score)


def plain_shards(
    activations,
    gate_weight,
    up_weight,
    out_grad,
    proj_in,
    proj_out,
    prompt_len,
    query_sketch,
    refusal_label,
):
    tok_rows = activations.shape[0]
    count = tok_rows // SEQ
    scaling = 1.0 / (4.0 * R)
    label_sign = (2 * refusal_label - 1).astype(jnp.bfloat16)
    out_part = jnp.dot(out_grad, proj_out, preferred_element_type=jnp.float32)
    whole_gate, whole_up = (
        lax.all_gather(gate_weight, "dp", axis=0, tiled=True),
        lax.all_gather(up_weight, "dp", axis=0, tiled=True),
    )
    block_cols = lax.all_gather(activations, "tp", axis=1, tiled=True)
    gate_sum = jnp.dot(block_cols, whole_gate, preferred_element_type=jnp.float32)
    up_sum = jnp.dot(block_cols, whole_up, preferred_element_type=jnp.float32)
    hidden = (jax.nn.silu(gate_sum) * up_sum).astype(jnp.bfloat16)
    in_part = jnp.dot(hidden, proj_in, preferred_element_type=jnp.float32)
    out_side, in_side = lax.psum((out_part, in_part), "tp")
    response = (jnp.arange(SEQ, dtype=jnp.int32)[None, :] >= prompt_len[:, None]).astype(
        jnp.float32
    )
    masked = out_side.reshape(count, SEQ, R) * response[:, :, None]
    sketch = jnp.einsum(
        "eti,etj->eij", masked, in_side.reshape(count, SEQ, R), precision=lax.Precision.HIGHEST
    )
    sketch = sketch.reshape(count, R * R).astype(jnp.bfloat16)
    scores = (
        lax.dot_general(
            sketch, query_sketch, (((1,), (1,)), ((), ())), preferred_element_type=jnp.float32
        )
        * scaling
    )
    local_terms = jnp.dot(scores, label_sign.astype(jnp.float32), precision=lax.Precision.HIGHEST)
    refusal_score = lax.psum(local_terms, "tp")
    refusal_score = refusal_score / jnp.sqrt(jnp.float32(NQ))
    return (scores, refusal_score)


def solution(mesh):
    body = shards if (mesh.shape["tp"], mesh.shape["dp"]) == (8, 2) else plain_shards
    return jax.shard_map(
        body,
        mesh=mesh,
        in_specs=(
            P(("groups", "dp"), "tp"),
            P("dp", "tp"),
            P("dp", "tp"),
            P(("groups", "dp"), "tp"),
            P("tp", None),
            P("tp", None),
            P(("groups", "dp")),
            P(("groups", "tp"), None),
            P(("groups", "tp")),
        ),
        out_specs=(P(("groups", "dp"), "tp"), P(("groups", "dp"))),
        check_vma=False,
    )
```

```python
import functools

import jax
import jax.numpy as jnp
from jax import lax
from jax.experimental import pallas as pl
from jax.experimental.pallas import tpu as pltpu
from jax.sharding import PartitionSpec as P

R = 64
SEQ = 32
NQ = 4096
MESH = pl.DeviceIdType.MESH
SCHEDULE = (
    ("pass", 0, 0),
    ("step", 0, 0),
    ("pass", 0, 1),
    ("step", 0, 1),
    ("wait", 2, 0),
    ("step", 2, 0),
    ("pass", 1, 0),
    ("wait", 2, 1),
    ("step", 2, 1),
    ("pass", 1, 1),
    ("step", 1, 0),
    ("step", 1, 1),
)
NB = 3


def layer_kernel(
    nt, tn, act, gate, up, pin, outw, query, lab,
    sk_out, v_out,
    A, acc, wbuf, sendb, part, rpart, skg, vself, vbuf,
    rsem, xsem, zsem, isem, psem, wsem, dsem, esem, tsem, trsem, gsem, grsem, vsem, vrsem, qsem, free,
):
    rows, feat = act.shape
    pr = rows // 2
    g = lax.axis_index("groups")
    t = lax.axis_index("tp")
    h = lax.axis_index("dp")
    z = t // 2
    x = t % 2
    u = z + h * (3 - 2 * z)
    v1 = jnp.minimum(u, 1)
    peer = (g, t, 1 - h)
    own = pl.multiple_of(h * rows, rows)
    oth = pl.multiple_of((1 - h) * rows, rows)

    def at_u(uu, xx):
        return (g, 2 * (uu + h * (3 - 2 * uu)) + xx, h)

    def ring(d):
        return (g, lax.rem(t + d, 8), h)

    def wcopies(w):
        s, j = w // (2 * nt), lax.rem(w, nt)
        v = v1 + (s // 2) * (1 - 2 * v1)
        kz = v + h * (1 - 2 * v)
        kx = x + (s % 2) * (1 - 2 * x)
        r0 = pl.multiple_of((kz * 2 + kx) * feat, feat)
        c0 = pl.multiple_of(j * tn, tn)
        b = lax.rem(w, NB)
        return [
            pltpu.make_async_copy(
                m.at[pl.ds(r0, feat), pl.ds(c0, tn)],
                wbuf.at[b, :, pl.ds(i * tn, tn)],
                wsem.at[b, i],
            )
            for i, m in enumerate((gate, up))
        ]

    def wstart(w):
        for c in wcopies(w):
            c.start()

    def qcopy(c):
        nq = query.shape[0]
        return pltpu.make_async_copy(
            query.at[:, pl.ds(c * feat, feat)],
            wbuf.at[1 + c // 2, pl.ds((c % 2) * nq, nq), :],
            qsem.at[c],
        )

    for c in range(4):
        qcopy(c).start()
    wstart(jnp.int32(0))

    barrier = pltpu.get_barrier_semaphore()
    for d in range(1, 8):
        pl.semaphore_signal(barrier, inc=1, device_id=ring(d), device_id_type=MESH)
    pl.semaphore_signal(barrier, inc=1, device_id=peer, device_id_type=MESH)
    pl.semaphore_wait(barrier, 8)

    def rcopy(src, dst, ss, rs, dev):
        return pltpu.make_async_remote_copy(
            src_ref=src, dst_ref=dst, send_sem=ss, recv_sem=rs, device_id=dev, device_id_type=MESH
        )

    def prow(p):
        half = (1 - h) + (p // 2) * (2 * h - 1)
        return pl.ds(pl.multiple_of(half * rows + (p % 2) * pr, pr), pr)

    def piece(s, p):
        return A.at[s, prow(p), :]

    inner = u <= 1

    def mine(i):
        return pltpu.make_async_copy(act.at[pl.ds(i * pr, pr), :], piece(0, 2 + i), rsem.at[0, 2 + i])

    def lend(i):
        dst = A.at[0, pl.ds(pl.multiple_of(h * rows + i * pr, pr), pr), :]
        return rcopy(act.at[pl.ds(i * pr, pr), :], dst, isem.at[i], rsem.at[0, i], peer)

    @pl.when(inner)
    def _():
        for i in range(2):
            mine(i).start()

    @pl.when(jnp.logical_not(inner))
    def _():
        for i in range(2):
            lend(i).start()

    def xfwd(s, p):
        return rcopy(
            piece(s, p), piece(s + 2, p), xsem.at[s, p], rsem.at[s + 2, p], at_u(u, 1 - x)
        )

    def zout(s, p):
        ds = jnp.where(u == 0, 1, 0) if s == 0 else 1
        return rcopy(piece(s, p), piece(ds, p), zsem.at[s, p], rsem.at[ds, p], at_u(u + 1, x))

    def zin(p):
        return rcopy(piece(0, p), piece(1, p), psem.at[p], rsem.at[1, p], at_u(u - 1, x))

    def out_ok(s):
        return (u <= 2) if s == 0 else jnp.logical_and(u >= 1, u <= 2)

    def arrived(s, p):
        rcopy(piece(s, p), piece(s, p), xsem.at[0, 0], rsem.at[s, p], peer).wait_recv()

    def forward(s, p):
        arrived(s, p)

        @pl.when(out_ok(s))
        def _():
            zout(s, p).start()

        if s == 0:

            @pl.when(u == 1)
            def _():
                zin(p).start()

        xfwd(s, p).start()

    nq = query.shape[0]
    sign = jnp.broadcast_to((2 * lab[...] - 1).astype(jnp.float32), (16, nq)).astype(jnp.bfloat16)
    for c in range(4):
        qcopy(c).wait()
        chunk = wbuf[1 + c // 2, pl.ds((c % 2) * nq, nq), :]
        signed = jnp.dot(sign, chunk, preferred_element_type=jnp.float32)
        vself[:, pl.ds(c * feat, feat)] = signed[:1]
    wstart(jnp.int32(1))
    for d in range(1, 8):
        rcopy(vself, vbuf.at[d], vsem.at[d], vrsem.at[d], ring(d)).start()

    part[...] = outw[...]

    def wready(w):
        for c in wcopies(w):
            c.wait()

        @pl.when(w + NB - 1 < 8 * nt)
        def _():
            wstart(w + NB - 1)

        return lax.rem(w, NB)

    def step(q, s, m):
        rs = pl.ds(own if m else oth, rows)

        def body(j, _):
            b = wready((2 * q + m) * nt + j)
            for i in range(2):
                cs = pl.ds(i * tn, tn)
                r = jnp.dot(A[s, rs, :], wbuf[b, :, cs], preferred_element_type=jnp.float32)
                if s == 0:
                    acc[j, rs, cs] = r
                else:
                    acc[j, rs, cs] += r
            return 0

        lax.fori_loop(0, nt, body, 0)

    def dsend(j):
        b = lax.rem(j, 2)
        return rcopy(
            sendb.at[b], acc.at[j, pl.ds(own, rows), :], dsem.at[b], esem.at[j], peer
        )

    for what, s, m in SCHEDULE:
        if what == "step":
            step((0, 2, 1)[s], s, m)
        else:
            for p in (2 * m, 2 * m + 1):
                (forward if what == "pass" else arrived)(s, p)

    for p in range(2):
        arrived(3, p)

    def give(j, _):
        b = wready(6 * nt + j)
        sb = lax.rem(j, 2)

        @pl.when(j >= 2)
        def _():
            dsend(j - 2).wait_send()

        for i in range(2):
            cs = pl.ds(i * tn, tn)
            sendb[sb, :, cs] = acc[j, pl.ds(oth, rows), cs] + jnp.dot(
                A[3, pl.ds(oth, rows), :], wbuf[b, :, cs], preferred_element_type=jnp.float32
            )
        pl.semaphore_signal(free, inc=1, device_id=peer, device_id_type=MESH)
        pl.semaphore_wait(free, 1)
        dsend(j).start()
        return 0

    lax.fori_loop(0, nt, give, 0)
    for p in range(2, 4):
        arrived(3, p)

    def take(j, _):
        b = wready(7 * nt + j)
        half = []
        rcopy(
            sendb.at[0], acc.at[j, pl.ds(oth, rows), :], dsem.at[0], esem.at[j], peer
        ).wait_recv()
        for i in range(2):
            cs = pl.ds(i * tn, tn)
            r = jnp.dot(
                A[3, pl.ds(own, rows), :], wbuf[b, :, cs], preferred_element_type=jnp.float32
            )
            half.append(r + acc[j, pl.ds(own, rows), cs] + acc[j, pl.ds(oth, rows), cs])
        gs, us = half
        hid = (gs / (1.0 + jnp.exp(-gs)) * us).astype(jnp.bfloat16)
        pj = pin[:, pl.ds(pl.multiple_of(j * tn, tn), tn)]
        part[:, :R] += lax.dot_general(
            hid, pj, (((1,), (1,)), ((), ())), preferred_element_type=jnp.float32
        )
        return 0

    lax.fori_loop(0, nt, take, 0)
    for j in range(nt - 2, nt):
        dsend(jnp.int32(j)).wait_send()

    share = rows // 8
    per = share // SEQ

    def scatter(d):
        dest = lax.rem(t + d, 8)
        src = part.at[pl.ds(pl.multiple_of(dest * share, share), share), :]
        return rcopy(src, rpart.at[d], tsem.at[d], trsem.at[d], ring(d))

    for d in range(1, 8):
        scatter(d).start()
    side = part[pl.ds(pl.multiple_of(t * share, share), share), :]
    for d in range(1, 8):
        scatter(d).wait_recv()
        side = side + rpart[d]
    for e in range(per):
        one = side[e * SEQ : (e + 1) * SEQ, :]
        gram = lax.dot_general(
            one, one, (((0,), (0,)), ((), ())),
            precision=lax.Precision.HIGHEST, preferred_element_type=jnp.float32,
        )
        skg[t * per + e] = gram[R:, :].astype(jnp.bfloat16)

    def spread(d):
        ref = skg.at[pl.ds(t * per, per)]
        return rcopy(ref, ref, gsem.at[d], grsem.at[d], ring(d))

    def landed(d):
        ref = skg.at[pl.ds(lax.rem(t + 8 - d, 8) * per, per)]
        rcopy(ref, ref, gsem.at[d], grsem.at[d], ring(d)).wait_recv()

    for d in range(1, 8):
        spread(d).start()
    total = vself[...]
    for d in range(1, 8):
        rcopy(vself, vbuf.at[d], vsem.at[d], vrsem.at[d], ring(d)).wait()
        total = total + vbuf[d]
    v_out[...] = total
    for s in range(2):
        for p in range(4):
            xfwd(s, p).wait_send()

            @pl.when(out_ok(s))
            def _():
                zout(s, p).wait_send()

            if s == 0:

                @pl.when(u == 1)
                def _():
                    zin(p).wait_send()

    @pl.when(jnp.logical_not(inner))
    def _():
        for i in range(2):
            lend(i).wait_send()

    for d in range(1, 8):
        scatter(d).wait_send()
    for d in range(1, 8):
        landed(d)
        spread(d).wait_send()
    sk_out[...] = skg[...]


def layer(act, gate, up, pin, outw, query, lab):
    rows, feat = act.shape
    ff = gate.shape[1]
    tn = 512
    nt = ff // tn
    count = rows // SEQ
    dma = pltpu.SemaphoreType.DMA
    vm = pl.BlockSpec(memory_space=pltpu.VMEM)
    hbm = pl.BlockSpec(memory_space=pl.ANY)
    return pl.pallas_call(
        functools.partial(layer_kernel, nt, tn),
        out_shape=(
            jax.ShapeDtypeStruct((count, R, 2 * R), jnp.bfloat16),
            jax.ShapeDtypeStruct((1, query.shape[1]), jnp.float32),
        ),
        in_specs=[hbm, hbm, hbm, vm, vm, hbm, vm],
        out_specs=(vm, vm),
        scratch_shapes=[
            pltpu.VMEM((4, 2 * rows, feat), jnp.bfloat16),
            pltpu.VMEM((nt, 2 * rows, 2 * tn), jnp.float32),
            pltpu.VMEM((NB, feat, 2 * tn), jnp.bfloat16),
            pltpu.VMEM((2, rows, 2 * tn), jnp.float32),
            pltpu.VMEM((rows, 2 * R), jnp.float32),
            pltpu.VMEM((8, rows // 8, 2 * R), jnp.float32),
            pltpu.VMEM((count, R, 2 * R), jnp.bfloat16),
            pltpu.VMEM((1, query.shape[1]), jnp.float32),
            pltpu.VMEM((8, 1, query.shape[1]), jnp.float32),
            dma((4, 4)), dma((2, 4)), dma((2, 4)), dma((2,)), dma((4,)), dma((NB, 2)),
            dma((2,)), dma((nt,)), dma((8,)), dma((8,)), dma((8,)), dma((8,)), dma((8,)), dma((8,)),
            dma((4,)), pltpu.SemaphoreType.REGULAR,
        ],
        compiler_params=pltpu.CompilerParams(
            collective_id=0, has_side_effects=True, vmem_limit_bytes=58 * 1024 * 1024
        ),
        cost_estimate=pl.CostEstimate(
            flops=8 * rows * gate.shape[0] * ff, bytes_accessed=8 * gate.shape[0] * ff,
            transcendentals=rows * ff,
        ),
    )(act, gate, up, pin, outw, query, lab)


def shards(
    activations,
    gate_weight,
    up_weight,
    out_grad,
    proj_in,
    proj_out,
    prompt_len,
    query_sketch,
    refusal_label,
):
    count = activations.shape[0] // SEQ
    scaling = 1.0 / (4.0 * R)
    response = (jnp.arange(SEQ, dtype=jnp.int32)[None, :] >= prompt_len[:, None]).astype(
        jnp.float32
    )
    wide_out = jnp.pad(proj_out, ((0, 0), (R, 0)))
    outw = jnp.dot(out_grad, wide_out, preferred_element_type=jnp.float32)
    outw = outw * response.reshape(-1, 1)
    sk, vsum = layer(
        activations, gate_weight, up_weight, proj_in.T, outw, query_sketch, refusal_label[None, :]
    )
    sketch = sk[:, :, :R].reshape(count, R * R)
    scores = (
        lax.dot_general(
            sketch, query_sketch, (((1,), (1,)), ((), ())), preferred_element_type=jnp.float32
        )
        * scaling
    )
    refusal_score = jnp.sum(sketch.astype(jnp.float32) * vsum.reshape(1, R * R), axis=1)
    refusal_score = refusal_score * (scaling / NQ**0.5)
    return (scores, refusal_score)


def plain_shards(
    activations,
    gate_weight,
    up_weight,
    out_grad,
    proj_in,
    proj_out,
    prompt_len,
    query_sketch,
    refusal_label,
):
    tok_rows = activations.shape[0]
    count = tok_rows // SEQ
    scaling = 1.0 / (4.0 * R)
    label_sign = (2 * refusal_label - 1).astype(jnp.bfloat16)
    out_part = jnp.dot(out_grad, proj_out, preferred_element_type=jnp.float32)
    whole_gate, whole_up = (
        lax.all_gather(gate_weight, "dp", axis=0, tiled=True),
        lax.all_gather(up_weight, "dp", axis=0, tiled=True),
    )
    block_cols = lax.all_gather(activations, "tp", axis=1, tiled=True)
    gate_sum = jnp.dot(block_cols, whole_gate, preferred_element_type=jnp.float32)
    up_sum = jnp.dot(block_cols, whole_up, preferred_element_type=jnp.float32)
    hidden = (jax.nn.silu(gate_sum) * up_sum).astype(jnp.bfloat16)
    in_part = jnp.dot(hidden, proj_in, preferred_element_type=jnp.float32)
    out_side, in_side = lax.psum((out_part, in_part), "tp")
    response = (jnp.arange(SEQ, dtype=jnp.int32)[None, :] >= prompt_len[:, None]).astype(
        jnp.float32
    )
    masked = out_side.reshape(count, SEQ, R) * response[:, :, None]
    sketch = jnp.einsum(
        "eti,etj->eij", masked, in_side.reshape(count, SEQ, R), precision=lax.Precision.HIGHEST
    )
    sketch = sketch.reshape(count, R * R).astype(jnp.bfloat16)
    scores = (
        lax.dot_general(
            sketch, query_sketch, (((1,), (1,)), ((), ())), preferred_element_type=jnp.float32
        )
        * scaling
    )
    local_terms = jnp.dot(scores, label_sign.astype(jnp.float32), precision=lax.Precision.HIGHEST)
    refusal_score = lax.psum(local_terms, "tp")
    refusal_score = refusal_score / jnp.sqrt(jnp.float32(NQ))
    return (scores, refusal_score)


def solution(mesh):
    body = shards if (mesh.shape["tp"], mesh.shape["dp"]) == (8, 2) else plain_shards
    return jax.shard_map(
        body,
        mesh=mesh,
        in_specs=(
            P(("groups", "dp"), "tp"),
            P("dp", "tp"),
            P("dp", "tp"),
            P(("groups", "dp"), "tp"),
            P("tp", None),
            P("tp", None),
            P(("groups", "dp")),
            P(("groups", "tp"), None),
            P(("groups", "tp")),
        ),
        out_specs=(P(("groups", "dp"), "tp"), P(("groups", "dp"))),
        check_vma=False,
    )
```
